512 devices in a mesh: chan: 8 (over y_hi, x), gx: 16 (over z), gy: 4 (over y_lo, core).
Axes of the slice: x: 4, y: 4 (y_hi: 2, y_lo: 2; y = y_hi * 2 + y_lo), z: 16, core: 2. Of those that a mesh axis runs over, the one named last changes fastest.
Arguments:
- features: bfloat16 [128, 32, 32, 128], P('chan', 'gx', 'gy'), may hold values from -6 to 6
- weight: bfloat16 [27, 128, 128], replicated, may hold values from -0.109375 to 0.109375
- bias: float32 [128], P('chan'), may hold values from -3 to 3
- cotangent: bfloat16 [128, 32, 32, 128], P('chan', 'gx', 'gy'), may hold values from -6 to 6
Outputs:
- output: bfloat16 [128, 32, 32, 128], P('chan', 'gx', 'gy')
- input_grad: bfloat16 [128, 32, 32, 128], P('chan', 'gx', 'gy')
- weight_grad: float32 [27, 128, 128], P(None, None, 'chan')
- bias_grad: float32 [128], P('chan')
The draws below stay inside these ranges and needn't reach their ends.
All inputs are finite; a program needn't handle non-finite values.
Results may differ from the reference program's by a relative error of at most 0.009.
Values may be sent and summed in bfloat16 or wider, within the bound.
No kernel may reach another device: no remote copies, remote signals or barrier semaphores. Data moves between devices by JAX's collectives and lax.ppermute only.
A program may use at most 64 MiB of HBM per device.

```python
import jax
import jax.numpy as jnp
from jax import lax

C = 128
NZ = 128
NX = 32
NY = 32


def block_levels(rng, dims, shards, low, top_value):
    gain = 1.0
    for position, parts in shards:
        draws = jax.random.uniform(jax.random.fold_in(jax.random.fold_in(rng, 6), position), (parts,), jnp.float32, low / len(shards), top_value / len(shards))
        gain = gain * jnp.repeat(jnp.exp(draws), dims[position] // parts).reshape((-1,) + (1,) * (len(dims) - 1 - position))
    return gain


def normal_values(rng, extent, spread, reach, shards=(), held_as=jnp.bfloat16):
    array = spread * jax.random.normal(rng, extent, jnp.float32)
    if shards:
        array = array * block_levels(rng, extent, shards, -0.22, 0.18)
    return jnp.clip(array, -reach, reach).astype(held_as)


def setup_inputs(seed: int = 0) -> dict:
    keys = jax.random.split(jax.random.key(seed), 5)
    return {
        "features": normal_values(keys[0], (C, NX, NY, NZ), 1.0, 6.0, ((0, 8), (1, 16), (2, 4))),
        "weight": normal_values(keys[1], (27, C, C), (27 * C) ** -0.5, 0.109375),
        "bias": normal_values(keys[2], (C,), 0.5, 3.0, ((0, 8),), jnp.float32),
        "cotangent": normal_values(keys[3], (C, NX, NY, NZ), 1.0, 6.0, ((0, 8), (1, 16), (2, 4))),
    }


def tap_offsets():
    found = []
    for first in range(3):
        for second in range(3):
            for third in range(3):
                found.append((first - 1, second - 1, third - 1))
    return found

def reference(features, weight, bias, cotangent):
    inputs = features.astype(jnp.float32)
    filters = weight.astype(jnp.float32)
    offsets = tap_offsets()
    pre = jnp.zeros(inputs.shape, jnp.float32) + bias[:, None, None, None]
    for index in range(27):
        dx, dy, dz = offsets[index]
        moved = jnp.roll(inputs, (-dx, -dy, -dz), axis=(1, 2, 3))
        pre = pre + jnp.einsum('oi,ixyz->oxyz', filters[index], moved)
    sigma = jax.nn.sigmoid(pre)
    output = (pre * sigma).astype(jnp.bfloat16)
    dpre = (cotangent.astype(jnp.float32) * sigma * (1.0 + pre * (1.0 - sigma))).astype(jnp.bfloat16)
    grads = dpre.astype(jnp.float32)
    input_grad = jnp.zeros(inputs.shape, jnp.float32)
    weight_rows = []
    scale = 1.0 / jnp.sqrt(jnp.float32(NX * NY * NZ))
    for index in range(27):
        dx, dy, dz = offsets[index]
        back = jnp.roll(grads, (dx, dy, dz), axis=(1, 2, 3))
        input_grad = input_grad + jnp.einsum('oi,oxyz->ixyz', filters[index], back)
        moved = jnp.roll(inputs, (-dx, -dy, -dz), axis=(1, 2, 3))
        weight_rows.append(jnp.einsum('oxyz,ixyz->oi', grads, moved))
    weight_grad = jnp.stack(weight_rows, axis=0) * scale
    bias_grad = lax.optimization_barrier(jnp.sum(grads, axis=(1, 2, 3))) * scale
    return (output, input_grad.astype(jnp.bfloat16), weight_grad, bias_grad)
```

```python
import functools

import jax
import jax.numpy as jnp
from jax import lax
from jax.experimental import pallas as pl
from jax.experimental.pallas import tpu as pltpu
from jax.sharding import Mesh, PartitionSpec as P

BF = jnp.bfloat16
F32 = jnp.float32
LANE = 128
TAPS = 27


def conv_kernel(place, got, weight, own_weight, out_ref, sums_ref, inner_ref, moved, grad, patch, spread, act):
    chan = place[0]
    gy = place[1]
    peers, _, chans, _ = got.shape
    width = peers * chans
    own = pl.multiple_of(chan * chans, chans)

    def row(index):
        return jnp.concatenate([got[p, index] for p in range(peers)], axis=0)

    for x in range(4):
        for y in range(10):
            tile = row(x * 10 + y)
            lanes = slice(y * LANE, (y + 1) * LANE)
            wide = tile.astype(F32)
            moved[x, 0:width, lanes] = pltpu.roll(wide, 1, 1).astype(BF)
            moved[x, width : 2 * width, lanes] = tile
            moved[x, 2 * width : 3 * width, lanes] = pltpu.roll(wide, LANE - 1, 1).astype(BF)

    bias = jnp.sum(row(56).astype(F32), axis=1, keepdims=True)
    filters = jnp.concatenate([weight[t] for t in range(TAPS)], axis=1)
    half = 4
    for x in range(2):
        for part in range(8 // half):
            y0 = part * half
            span = half * LANE
            cells = jnp.concatenate(
                [moved[x + a, :, (b + y0) * LANE : (b + y0) * LANE + span] for a in range(3) for b in range(3)],
                axis=0,
            )
            pre = jnp.dot(filters, cells, preferred_element_type=F32) + bias
            sigma = jax.nn.sigmoid(pre)
            cot = jnp.concatenate([row(40 + x * 8 + y0 + y) for y in range(half)], axis=1).astype(F32)
            lanes = slice((x * 8 + y0) * LANE, (x * 8 + y0) * LANE + span)
            grad[:, lanes] = (cot * sigma * (1.0 + pre * (1.0 - sigma))).astype(BF)
            act[:, lanes] = (pre * sigma).astype(BF)
    for x in range(2):
        for y in range(8):
            lanes = slice((x * 8 + y) * LANE, (x * 8 + y + 1) * LANE)
            out_ref[x, y] = act[pl.ds(own, chans), lanes]

    for a in range(3):
        for b in range(3):
            for c in range(3):
                t = 9 * a + 3 * b + c
                for x in range(2):
                    patch[t * chans : (t + 1) * chans, x * 1024 : (x + 1) * 1024] = moved[
                        x + a, pl.ds(pl.multiple_of(c * width + own, chans), chans), b * LANE : (b + 8) * LANE
                    ]
    index = lax.broadcasted_iota(jnp.int32, (chans, 2048), 0)
    patch[TAPS * chans :, :] = jnp.where(index == 0, 1.0, 0.0).astype(BF)
    total = lax.dot_general(patch[...], grad[...], (((1,), (1,)), ((), ())), preferred_element_type=F32)
    quarter = total.shape[0] // 4
    for g in range(4):
        sums_ref[g, 0:quarter, :] = total[g * quarter : (g + 1) * quarter]
        sums_ref[g, quarter:, :] = jnp.zeros((4 * chans, LANE), F32)

    spread[...] = jnp.zeros(spread.shape, F32)
    for x in range(2):
        terms = jnp.dot(own_weight[...], grad[:, x * 1024 : (x + 1) * 1024], preferred_element_type=F32)
        for a in range(3):
            for b in range(3):
                for c in range(3):
                    t = 9 * a + 3 * b + c
                    spread[c, x + a, :, b * LANE : (b + 8) * LANE] += terms[t * chans : (t + 1) * chans]
    after = lax.rem(gy + 1, 4)
    before = lax.rem(gy + 3, 4)
    for x in range(4):
        for y in range(10):
            lanes = slice(y * LANE, (y + 1) * LANE)
            tile = (
                pltpu.roll(spread[0, x, :, lanes], LANE - 1, 1)
                + spread[1, x, :, lanes]
                + pltpu.roll(spread[2, x, :, lanes], 1, 1)
            )
            spot = slice(quarter + x * chans, quarter + (x + 1) * chans)
            if y == 0:
                sums_ref[before, spot, :] = tile
            elif y == 9:
                sums_ref[after, spot, :] = tile
            else:
                inner_ref[x, y - 1] = tile


def on_device(features, weight, bias, cotangent):
    chans, extent_x, extent_y, depth = features.shape
    width = weight.shape[1]
    peers = width // chans
    chan = lax.axis_index("chan")
    gy = lax.axis_index("gy")
    count_x = lax.axis_size("zh") * lax.axis_size("zl")
    count_y = lax.axis_size("gy")
    gx_axes = ("zh", "zl")
    up = [(i, (i + 1) % count_x) for i in range(count_x)]
    down = [(i, (i - 1) % count_x) for i in range(count_x)]
    after = lax.rem(gy + 1, count_y)
    before = lax.rem(gy + count_y - 1, count_y)
    slot = lax.broadcasted_iota(jnp.int32, (count_y, 1, 1, 1), 0)

    rows = jnp.transpose(features, (1, 2, 0, 3))
    low = lax.ppermute(rows[-1:], gx_axes, up)
    high = lax.ppermute(rows[:1], gx_axes, down)
    own_weight = lax.dynamic_slice_in_dim(weight, chan * chans, chans, 2)
    own_weight = jnp.transpose(own_weight, (0, 2, 1)).reshape(TAPS * chans, width)
    cot_rows = jnp.transpose(cotangent, (1, 2, 0, 3)).reshape(extent_x * extent_y, chans, depth)
    first = lax.reduce_precision(bias, 8, 7)
    second = lax.reduce_precision(bias - first, 8, 7)
    third = bias - first - second
    bias_row = jnp.stack([first, second, third], axis=1).astype(BF)
    bias_row = jnp.pad(bias_row, ((0, 0), (0, depth - 3)))[None]

    rows = jnp.concatenate([low, rows, high], axis=0)
    edges = jnp.where(slot == after, rows[None, :, -1], jnp.where(slot == before, rows[None, :, 0], 0)).astype(BF)
    edges = lax.all_to_all(edges, "gy", 0, 0)
    south = lax.dynamic_index_in_dim(edges, before, 0, keepdims=False)
    north = lax.dynamic_index_in_dim(edges, after, 0, keepdims=False)
    rows = jnp.concatenate([south[:, None], rows, north[:, None]], axis=1)
    parcel = jnp.concatenate([rows.reshape(-1, chans, depth), cot_rows, bias_row], axis=0)
    got = lax.all_to_all(jnp.broadcast_to(parcel, (peers,) + parcel.shape), "chan", 0, 0)

    cells = extent_x * extent_y * depth
    piece = (TAPS + 1) * chans // 4
    vmem = pl.BlockSpec(memory_space=pltpu.VMEM)
    output, sums, inner = pl.pallas_call(
        conv_kernel,
        out_shape=(
            jax.ShapeDtypeStruct((extent_x, extent_y, chans, depth), BF),
            jax.ShapeDtypeStruct((4, piece + 4 * chans, LANE), F32),
            jax.ShapeDtypeStruct((4, extent_y, chans, depth), F32),
        ),
        in_specs=[pl.BlockSpec(memory_space=pltpu.SMEM), vmem, vmem, vmem],
        out_specs=(vmem, vmem, vmem),
        scratch_shapes=[
            pltpu.VMEM((4, 3 * width, 10 * LANE), BF),
            pltpu.VMEM((width, cells), BF),
            pltpu.VMEM(((TAPS + 1) * chans, cells), BF),
            pltpu.VMEM((3, 4, chans, 10 * LANE), F32),
            pltpu.VMEM((width, cells), BF),
        ],
        compiler_params=pltpu.CompilerParams(vmem_limit_bytes=40 * 1024 * 1024),
    )(jnp.stack([chan, gy]).astype(jnp.int32), got, weight, own_weight)

    sums = lax.all_to_all(sums, "gy", 0, 0)
    edge = sums[:, piece:].reshape(4, 4, chans, depth)
    south = lax.dynamic_index_in_dim(edge, before, 0, keepdims=False)
    north = lax.dynamic_index_in_dim(edge, after, 0, keepdims=False)
    inner = jnp.concatenate([inner[:, :1] + south[:, None], inner[:, 1:-1], inner[:, -1:] + north[:, None]], axis=1)
    low = lax.ppermute(inner[-1:], gx_axes, up)
    high = lax.ppermute(inner[:1], gx_axes, down)
    scale = 1.0 / jnp.sqrt(jnp.float32(count_x * count_y * cells))
    part = jnp.sum(sums[:, :piece], axis=0).astype(BF)
    part = lax.all_to_all(jnp.broadcast_to(part, (4,) + part.shape), "zl", 0, 0)
    part = jnp.sum(part.astype(F32), axis=0).astype(BF)
    part = lax.all_to_all(jnp.broadcast_to(part, (4,) + part.shape), "zh", 0, 0)
    part = (jnp.sum(part.astype(F32), axis=0) * scale).astype(BF)
    part = lax.all_to_all(jnp.broadcast_to(part, (4,) + part.shape), "gy", 0, 0)
    whole = part.reshape((TAPS + 1) * chans, LANE).astype(F32)
    weight_grad = jnp.transpose(whole[: TAPS * chans].reshape(TAPS, chans, width), (0, 2, 1))
    bias_grad = lax.dynamic_slice_in_dim(whole[TAPS * chans], chan * chans, chans, 0)

    input_grad = jnp.concatenate([inner[1:2] + low, inner[2:3] + high], axis=0).astype(BF)
    return (
        jnp.transpose(output, (2, 0, 1, 3)),
        jnp.transpose(input_grad, (2, 0, 1, 3)),
        weight_grad,
        bias_grad,
    )


def solution(mesh):
    split = Mesh(mesh.devices.reshape(8, 4, 4, 4), ("chan", "zh", "zl", "gy"))
    block = P("chan", ("zh", "zl"), "gy", None)
    return jax.shard_map(
        on_device,
        mesh=split,
        in_specs=(block, P(), P("chan"), block),
        out_specs=(block, block, P(None, None, "chan"), P("chan")),
        check_vma=False,
    )
```

```python
import functools

import jax
import jax.numpy as jnp
from jax import lax
from jax.experimental import pallas as pl
from jax.experimental.pallas import tpu as pltpu
from jax.sharding import Mesh, PartitionSpec as P

BF = jnp.bfloat16
F32 = jnp.float32
LANE = 128
TAPS = 27


def pack_block(features, cotangent, out, first, last):
    peers = out.shape[0]
    extent_x, extent_y = features.shape[1:3]
    for array, start in ((features, 0), (cotangent, extent_x * extent_y)):
        for x in range(extent_x):
            rows = jnp.swapaxes(array[:, x].astype(F32), 0, 1).astype(BF)
            for p in range(peers):
                out[p, start + x * extent_y : start + (x + 1) * extent_y] = rows
            if start == 0 and x == 0:
                first[...] = rows
            if start == 0 and x == extent_x - 1:
                last[...] = rows


def pack_layer(low, high, south, north, bias, out):
    for p in range(out.shape[0]):
        out[p, 0:8] = low[...]
        out[p, 8:16] = high[...]
        out[p, 16:20] = south[...]
        out[p, 20:24] = north[...]
        out[p, 24:25] = bias[...]


def sum_parts(scale, parts, out):
    total = jnp.sum(parts[...].astype(F32), axis=0)
    if scale != 1.0:
        total = total * jnp.float32(scale)
    for p in range(out.shape[0]):
        out[p] = total.astype(BF)


def unpack_sums(place, parts, weight_out, bias_out):
    piece = parts.shape[1]
    rows, width = weight_out.shape
    chans = bias_out.shape[1]
    for n in range(parts.shape[0]):
        start = n * piece
        values = parts[n].astype(F32)
        if start + piece <= rows:
            weight_out[start : start + piece] = values
        elif start <= rows:
            if start < rows:
                weight_out[start:rows] = values[: rows - start]
            line = values[rows - start : rows - start + 1]
            bias_out[...] = pltpu.roll(line, lax.rem(width - place[0] * chans, width), 1)[:, :chans]


def conv_kernel(
    place, got, halo, weight, own_weight, out_ref, sums_ref, inner_ref, edge_ref, moved, grad, patch, spread, act
):
    chan = place[0]
    peers, _, chans, _ = got.shape
    width = peers * chans
    own = pl.multiple_of(chan * chans, chans)

    def row(index, ref=got):
        return jnp.concatenate([ref[p, index] for p in range(peers)], axis=0)

    def feature(x, y):
        if y == 0 or y == 9:
            return row(16 + (y // 9) * 4 + x, halo)
        if x == 0 or x == 3:
            return row((x // 3) * 8 + y - 1, halo)
        return row((x - 1) * 8 + y - 1)

    for x in range(4):
        for y in range(10):
            tile = feature(x, y)
            lanes = slice(y * LANE, (y + 1) * LANE)
            wide = tile.astype(F32)
            moved[x, 0:width, lanes] = pltpu.roll(wide, 1, 1).astype(BF)
            moved[x, width : 2 * width, lanes] = tile
            moved[x, 2 * width : 3 * width, lanes] = pltpu.roll(wide, LANE - 1, 1).astype(BF)

    bias = jnp.sum(row(24, halo).astype(F32), axis=1, keepdims=True)
    filters = jnp.concatenate([weight[t] for t in range(TAPS)], axis=1)
    half = 4
    for x in range(2):
        for part in range(8 // half):
            y0 = part * half
            span = half * LANE
            cells = jnp.concatenate(
                [moved[x + a, :, (b + y0) * LANE : (b + y0) * LANE + span] for a in range(3) for b in range(3)],
                axis=0,
            )
            pre = jnp.dot(filters, cells, preferred_element_type=F32) + bias
            sigma = jax.nn.sigmoid(pre)
            cot = jnp.concatenate([row(16 + x * 8 + y0 + y) for y in range(half)], axis=1).astype(F32)
            lanes = slice((x * 8 + y0) * LANE, (x * 8 + y0) * LANE + span)
            grad[:, lanes] = (cot * sigma * (1.0 + pre * (1.0 - sigma))).astype(BF)
            act[:, lanes] = (pre * sigma).astype(BF)
    for x in range(2):
        for y in range(8):
            lanes = slice((x * 8 + y) * LANE, (x * 8 + y + 1) * LANE)
            out_ref[x, y] = act[pl.ds(own, chans), lanes]

    for a in range(3):
        for b in range(3):
            for c in range(3):
                t = 9 * a + 3 * b + c
                for x in range(2):
                    patch[t * chans : (t + 1) * chans, x * 1024 : (x + 1) * 1024] = moved[
                        x + a, pl.ds(pl.multiple_of(c * width + own, chans), chans), b * LANE : (b + 8) * LANE
                    ]
    spare = patch.shape[0] - TAPS * chans
    index = lax.broadcasted_iota(jnp.int32, (spare, patch.shape[1]), 0)
    patch[TAPS * chans :, :] = jnp.where(index == 0, 1.0, 0.0).astype(BF)
    sums_ref[...] = lax.dot_general(
        patch[...], grad[...], (((1,), (1,)), ((), ())), preferred_element_type=F32
    ).astype(BF)

    spread[...] = jnp.zeros(spread.shape, F32)
    for x in range(2):
        terms = jnp.dot(own_weight[...], grad[:, x * 1024 : (x + 1) * 1024], preferred_element_type=F32)
        for a in range(3):
            for b in range(3):
                for c in range(3):
                    t = 9 * a + 3 * b + c
                    spread[c, x + a, :, b * LANE : (b + 8) * LANE] += terms[t * chans : (t + 1) * chans]
    for x in range(4):
        for y in range(10):
            lanes = slice(y * LANE, (y + 1) * LANE)
            tile = (
                pltpu.roll(spread[0, x, :, lanes], LANE - 1, 1)
                + spread[1, x, :, lanes]
                + pltpu.roll(spread[2, x, :, lanes], 1, 1)
            )
            if y == 0 or y == 9:
                edge_ref[y // 9, x] = tile
            else:
                inner_ref[x, y - 1] = tile


def on_device(features, weight, bias, cotangent):
    chans, extent_x, extent_y, depth = features.shape
    width = weight.shape[1]
    peers = width // chans
    chan = lax.axis_index("chan")
    count_x = lax.axis_size("zh") * lax.axis_size("zl")
    count_y = lax.axis_size("gy")
    gx_axes = ("zh", "zl")
    up = [(i, (i + 1) % count_x) for i in range(count_x)]
    down = [(i, (i - 1) % count_x) for i in range(count_x)]

    vmem = pl.BlockSpec(memory_space=pltpu.VMEM)
    smem = pl.BlockSpec(memory_space=pltpu.SMEM)

    def call(body, out_shape, *operands, specs=None):
        return pl.pallas_call(
            body,
            out_shape=out_shape,
            in_specs=specs or [vmem] * len(operands),
            out_specs=jax.tree.map(lambda _: vmem, out_shape),
            compiler_params=pltpu.CompilerParams(vmem_limit_bytes=16 * 1024 * 1024),
        )(*operands)

    plane = jax.ShapeDtypeStruct((extent_y, chans, depth), BF)
    parcel, x_first, x_last = call(
        pack_block,
        (jax.ShapeDtypeStruct((peers, 2 * extent_x * extent_y, chans, depth), BF), plane, plane),
        features,
        cotangent,
    )
    got = lax.all_to_all(parcel, "chan", 0, 0)

    low = lax.ppermute(x_last, gx_axes, up)
    high = lax.ppermute(x_first, gx_axes, down)
    right = [(i, (i + 1) % count_y) for i in range(count_y)]
    left = [(i, (i - 1) % count_y) for i in range(count_y)]
    south = lax.ppermute(jnp.stack([low[-1], x_first[-1], x_last[-1], high[-1]]), "gy", right)
    north = lax.ppermute(jnp.stack([low[0], x_first[0], x_last[0], high[0]]), "gy", left)
    first = lax.reduce_precision(bias, 8, 7)
    second = lax.reduce_precision(bias - first, 8, 7)
    third = bias - first - second
    bias_row = jnp.stack([first, second, third], axis=1).astype(BF)
    bias_row = jnp.pad(bias_row, ((0, 0), (0, depth - 3)))[None]
    parcel = call(
        pack_layer,
        jax.ShapeDtypeStruct((peers, 2 * extent_y + 9, chans, depth), BF),
        low,
        high,
        south,
        north,
        bias_row,
    )
    parcel, got = lax.optimization_barrier((parcel, got))
    halo = lax.all_to_all(parcel, "chan", 0, 0)
    own_weight = lax.dynamic_slice_in_dim(weight, chan * chans, chans, 2)
    own_weight = jnp.transpose(own_weight, (0, 2, 1)).reshape(TAPS * chans, width)

    cells = extent_x * extent_y * depth
    near = lax.axis_size("zl") * count_y
    piece = -(-(TAPS * chans + 1) // (near * 16)) * 16
    place = chan.astype(jnp.int32).reshape(1)
    output, sums, inner, edge = pl.pallas_call(
        conv_kernel,
        out_shape=(
            jax.ShapeDtypeStruct((extent_x, extent_y, chans, depth), BF),
            jax.ShapeDtypeStruct((near * piece, width), BF),
            jax.ShapeDtypeStruct((4, extent_y, chans, depth), F32),
            jax.ShapeDtypeStruct((2, 4, chans, depth), F32),
        ),
        in_specs=[smem, vmem, vmem, vmem, vmem],
        out_specs=(vmem, vmem, vmem, vmem),
        scratch_shapes=[
            pltpu.VMEM((4, 3 * width, 10 * LANE), BF),
            pltpu.VMEM((width, cells), BF),
            pltpu.VMEM((near * piece, cells), BF),
            pltpu.VMEM((3, 4, chans, 10 * LANE), F32),
            pltpu.VMEM((width, cells), BF),
        ],
        compiler_params=pltpu.CompilerParams(vmem_limit_bytes=40 * 1024 * 1024),
    )(place, got, halo, weight, own_weight)

    scale = 1.0 / float(count_x * count_y * cells) ** 0.5
    far = lax.axis_size("zh")
    part = lax.all_to_all(sums.reshape(near, piece, width), ("zl", "gy"), 0, 0)
    north = lax.ppermute(edge[0], "gy", left)
    south = lax.ppermute(edge[1], "gy", right)
    part = call(functools.partial(sum_parts, 1.0), jax.ShapeDtypeStruct((far, piece, width), BF), part)
    part = lax.all_to_all(part, "zh", 0, 0)
    inner = jnp.concatenate([inner[:, :1] + south[:, None], inner[:, 1:-1], inner[:, -1:] + north[:, None]], axis=1)
    low = lax.ppermute(inner[-1:], gx_axes, up)
    high = lax.ppermute(inner[:1], gx_axes, down)
    part, low, high = lax.optimization_barrier((part, low, high))
    part = call(functools.partial(sum_parts, scale), jax.ShapeDtypeStruct((near, piece, width), BF), part)
    part = lax.all_to_all(part, ("zl", "gy"), 0, 0)
    whole, bias_grad = call(
        unpack_sums,
        (jax.ShapeDtypeStruct((TAPS * chans, width), F32), jax.ShapeDtypeStruct((1, chans), F32)),
        place,
        part,
        specs=[smem, vmem],
    )
    weight_grad = jnp.transpose(whole.reshape(TAPS, chans, width), (0, 2, 1))
    input_grad = jnp.concatenate([inner[1:2] + low, inner[2:3] + high], axis=0).astype(BF)
    return (
        jnp.transpose(output, (2, 0, 1, 3)),
        jnp.transpose(input_grad, (2, 0, 1, 3)),
        weight_grad,
        bias_grad.reshape(chans),
    )


def solution(mesh):
    split = Mesh(mesh.devices.reshape(8, 4, 4, 4), ("chan", "zh", "zl", "gy"))
    block = P("chan", ("zh", "zl"), "gy", None)
    return jax.shard_map(
        on_device,
        mesh=split,
        in_specs=(block, P(), P("chan"), block),
        out_specs=(block, block, P(None, None, "chan"), P("chan")),
        check_vma=False,
    )
```

```python
import functools

import jax
import jax.numpy as jnp
from jax import lax
from jax.experimental import pallas as pl
from jax.experimental.pallas import tpu as pltpu
from jax.sharding import Mesh, PartitionSpec as P

BF = jnp.bfloat16
F32 = jnp.float32
LANE = 128
TAPS = 27


def pack_block(features_hbm, cotangent_hbm, bias_hbm, out, x_send, y_send, features, cotangent, bias, arrived):
    copies = [
        pltpu.make_async_copy(source, target, arrived.at[n])
        for n, (source, target) in enumerate(
            ((features_hbm, features), (cotangent_hbm, cotangent), (bias_hbm, bias))
        )
    ]
    for copy in copies:
        copy.start()
    for copy in copies:
        copy.wait()
    cells = 2 * 8
    for x in range(2):
        rows = jnp.swapaxes(features[:, x].astype(F32), 0, 1).astype(BF)
        x_send[x * 8 : (x + 1) * 8] = rows
        y_send[2 * x : 2 * x + 2] = rows[0:2]
        for p in range(out.shape[0]):
            out[p, x * 8 : (x + 1) * 8] = rows
    x_send[cells:] = jnp.swapaxes(cotangent[:, 0].astype(F32), 0, 1).astype(BF)
    rows = jnp.swapaxes(cotangent[:, 1].astype(F32), 0, 1).astype(BF)
    y_send[4:5] = rows[0:1]
    chans = bias.shape[1]
    line = lax.broadcasted_iota(jnp.int32, (chans, chans), 0)
    lane = lax.broadcasted_iota(jnp.int32, (chans, chans), 1)
    column = jnp.sum(jnp.where(line == lane, jnp.broadcast_to(bias[...], (chans, chans)), 0.0), axis=1, keepdims=True)
    first = column.astype(BF).astype(F32)
    second = (column - first).astype(BF).astype(F32)
    third = column - first - second
    lane = lax.broadcasted_iota(jnp.int32, (chans, LANE), 1)
    parts = jnp.where(lane == 0, first, jnp.where(lane == 1, second, jnp.where(lane == 2, third, 0.0)))
    for p in range(out.shape[0]):
        out[p, cells] = parts.astype(BF)
        out[p, cells + 1 :] = rows[1:]


def pack_edge(own, from_x, out):
    out[0:4] = own[0:4]
    out[4:6] = from_x[0:2]
    out[6:8] = from_x[8:10]
    out[8:9] = own[4:5]
    out[9:10] = from_x[16:17]


def pack_layer(from_x, from_y, out):
    for p in range(out.shape[0]):
        out[p, 0:16] = from_x[0:16]
        out[p, 16:23] = from_x[17:24]
        out[p, 23:33] = from_y[...]


def add_edge(inner, from_y, keep, send):
    for plane in range(6):
        grad_plane = plane < 4
        rows = 2 if grad_plane else 1
        start = 2 * plane if grad_plane else 8 + plane - 4
        values = inner[plane]
        added = from_y[start : start + rows].astype(F32)
        values = jnp.concatenate([values[0:rows] + added, values[rows:]], axis=0)
        if plane in (0, 1, 4):
            keep[min(plane, 2)] = values
        else:
            send[min(plane - 2, 2)] = values.astype(BF)


def finish(keep, from_x, output, input_grad):
    for x in range(2):
        input_grad[:, x] = jnp.swapaxes(keep[x] + from_x[x].astype(F32), 0, 1).astype(BF)
    output[:, 0] = jnp.swapaxes(from_x[2].astype(F32), 0, 1).astype(BF)
    output[:, 1] = jnp.swapaxes(keep[2], 0, 1).astype(BF)


def sum_parts(scale, parts, out):
    total = jnp.sum(parts[...].astype(F32), axis=0)
    if scale != 1.0:
        total = total * jnp.float32(scale)
    for p in range(out.shape[0]):
        out[p] = total.astype(BF)


def unpack_sums(place, parts, weight_out, bias_out):
    piece = parts.shape[1]
    rows, width = weight_out.shape
    chans = bias_out.shape[1]
    for n in range(parts.shape[0]):
        start = n * piece
        values = parts[n].astype(F32)
        if start + piece <= rows:
            weight_out[start : start + piece] = values
        elif start <= rows:
            if start < rows:
                weight_out[start:rows] = values[: rows - start]
            line = values[rows - start : rows - start + 1]
            bias_out[...] = pltpu.roll(line, lax.rem(width - place[0] * chans, width), 1)[:, :chans]


def conv_kernel(place, got, layer, weight, own_weight, sums_ref, inner_ref, edge_ref, moved, grad, patch, spread, act):
    chan = place[0]
    peers, _, chans, _ = got.shape
    width = peers * chans
    own = pl.multiple_of(chan * chans, chans)

    def row(ref, index):
        return jnp.concatenate([ref[p, index] for p in range(peers)], axis=0)

    def feature(x, y):
        if y >= 8:
            return row(layer, 23 + 2 * x + y - 8)
        return row(got, x * 8 + y) if x < 2 else row(layer, (x - 2) * 8 + y)

    def cotangent(x, y):
        if y == 7:
            return row(layer, 31 + x)
        return row(layer, 16 + y) if x else row(got, 17 + y)

    for x in range(4):
        for y in range(10):
            tile = feature(x, y)
            lanes = slice(y * LANE, (y + 1) * LANE)
            wide = tile.astype(F32)
            moved[x, 0:width, lanes] = pltpu.roll(wide, 1, 1).astype(BF)
            moved[x, width : 2 * width, lanes] = tile
            moved[x, 2 * width : 3 * width, lanes] = pltpu.roll(wide, LANE - 1, 1).astype(BF)

    bias = jnp.sum(row(got, 16).astype(F32), axis=1, keepdims=True)
    filters = jnp.concatenate([weight[t] for t in range(TAPS)], axis=1)
    half = 4
    for x in range(2):
        for part in range(8 // half):
            y0 = part * half
            span = half * LANE
            cells = jnp.concatenate(
                [moved[x + a, :, (b + y0) * LANE : (b + y0) * LANE + span] for a in range(3) for b in range(3)],
                axis=0,
            )
            pre = jnp.dot(filters, cells, preferred_element_type=F32) + bias
            sigma = jax.nn.sigmoid(pre)
            cot = jnp.concatenate([cotangent(x, y0 + y) for y in range(half)], axis=1).astype(F32)
            lanes = slice((x * 8 + y0) * LANE, (x * 8 + y0) * LANE + span)
            grad[:, lanes] = (cot * sigma * (1.0 + pre * (1.0 - sigma))).astype(BF)
            act[:, lanes] = (pre * sigma).astype(BF)
    for x in range(2):
        inner_ref[4 + x, 0] = jnp.zeros((chans, LANE), F32)
        for y in range(8):
            lanes = slice((x * 8 + y) * LANE, (x * 8 + y + 1) * LANE)
            tile = act[pl.ds(own, chans), lanes]
            if y == 7:
                edge_ref[8 + x] = tile
            else:
                inner_ref[4 + x, y + 1] = tile.astype(F32)

    for a in range(3):
        for b in range(3):
            for c in range(3):
                t = 9 * a + 3 * b + c
                for x in range(2):
                    patch[t * chans : (t + 1) * chans, x * 1024 : (x + 1) * 1024] = moved[
                        x + a, pl.ds(pl.multiple_of(c * width + own, chans), chans), b * LANE : (b + 8) * LANE
                    ]
    spare = patch.shape[0] - TAPS * chans
    index = lax.broadcasted_iota(jnp.int32, (spare, patch.shape[1]), 0)
    patch[TAPS * chans :, :] = jnp.where(index == 0, 1.0, 0.0).astype(BF)
    sums_ref[...] = lax.dot_general(
        patch[...], grad[...], (((1,), (1,)), ((), ())), preferred_element_type=F32
    ).astype(BF)

    spread[...] = jnp.zeros(spread.shape, F32)
    for x in range(2):
        terms = jnp.dot(own_weight[...], grad[:, x * 1024 : (x + 1) * 1024], preferred_element_type=F32)
        for a in range(3):
            for b in range(3):
                for c in range(3):
                    t = 9 * a + 3 * b + c
                    spread[c, x + a, :, b * LANE : (b + 8) * LANE] += terms[t * chans : (t + 1) * chans]
    for x in range(4):
        for y in range(10):
            lanes = slice(y * LANE, (y + 1) * LANE)
            tile = (
                pltpu.roll(spread[0, x, :, lanes], LANE - 1, 1)
                + spread[1, x, :, lanes]
                + pltpu.roll(spread[2, x, :, lanes], 1, 1)
            )
            if y >= 8:
                edge_ref[2 * x + y - 8] = tile.astype(BF)
            else:
                inner_ref[x, y] = tile


def on_device(features, weight, bias, cotangent):
    chans, extent_x, extent_y, depth = features.shape
    width = weight.shape[1]
    peers = width // chans
    chan = lax.axis_index("chan")
    count_x = lax.axis_size("zh") * lax.axis_size("zl")
    count_y = lax.axis_size("gy")
    gx_axes = ("zh", "zl")
    up = [(i, (i + 1) % count_x) for i in range(count_x)]
    down = [(i, (i - 1) % count_x) for i in range(count_x)]

    vmem = pl.BlockSpec(memory_space=pltpu.VMEM)
    smem = pl.BlockSpec(memory_space=pltpu.SMEM)

    def call(body, out_shape, *operands, specs=None):
        return pl.pallas_call(
            body,
            out_shape=out_shape,
            in_specs=specs or [vmem] * len(operands),
            out_specs=jax.tree.map(lambda _: vmem, out_shape),
            compiler_params=pltpu.CompilerParams(vmem_limit_bytes=16 * 1024 * 1024),
        )(*operands)

    def rows_of(*shape, dtype=BF):
        return jax.ShapeDtypeStruct((*shape, chans, depth), dtype)

    anywhere = pl.BlockSpec(memory_space=pl.ANY)
    parcel, x_send, y_send = pl.pallas_call(
        pack_block,
        out_shape=(rows_of(peers, 24), rows_of(24), rows_of(5)),
        in_specs=[anywhere] * 3,
        out_specs=(vmem,) * 3,
        scratch_shapes=[
            pltpu.VMEM(features.shape, BF),
            pltpu.VMEM(features.shape, BF),
            pltpu.VMEM((1, chans), F32),
            pltpu.SemaphoreType.DMA((3,)),
        ],
        compiler_params=pltpu.CompilerParams(vmem_limit_bytes=60 * 1024 * 1024),
    )(features, cotangent, bias.reshape(1, chans))
    got = lax.all_to_all(parcel, "chan", 0, 0)

    forth = [(i, (i + 1) % count_y) for i in range(count_y)]
    back = [(i, (i - 1) % count_y) for i in range(count_y)]
    from_x = lax.ppermute(x_send, gx_axes, down)
    from_y = lax.ppermute(call(pack_edge, rows_of(10), y_send, from_x), "gy", back)
    parcel = call(pack_layer, rows_of(peers, 33), from_x, from_y)
    parcel, got = lax.optimization_barrier((parcel, got))
    layer = lax.all_to_all(parcel, "chan", 0, 0)
    own_weight = lax.dynamic_slice_in_dim(weight, chan * chans, chans, 2)
    own_weight = jnp.transpose(own_weight, (0, 2, 1)).reshape(TAPS * chans, width)

    cells = extent_x * extent_y * depth
    near = lax.axis_size("zl") * count_y
    piece = -(-(TAPS * chans + 1) // (near * 16)) * 16
    place = chan.astype(jnp.int32).reshape(1)
    sums, inner, edge = pl.pallas_call(
        conv_kernel,
        out_shape=(
            jax.ShapeDtypeStruct((near * piece, width), BF),
            rows_of(6, extent_y, dtype=F32),
            rows_of(10),
        ),
        in_specs=[smem, vmem, vmem, vmem, vmem],
        out_specs=(vmem, vmem, vmem),
        scratch_shapes=[
            pltpu.VMEM((4, 3 * width, 10 * LANE), BF),
            pltpu.VMEM((width, cells), BF),
            pltpu.VMEM((near * piece, cells), BF),
            pltpu.VMEM((3, 4, chans, 10 * LANE), F32),
            pltpu.VMEM((width, cells), BF),
        ],
        compiler_params=pltpu.CompilerParams(vmem_limit_bytes=40 * 1024 * 1024),
    )(place, got, layer, weight, own_weight)

    scale = 1.0 / float(count_x * count_y * cells) ** 0.5
    far = lax.axis_size("zh")
    run = lax.axis_size("zl")
    middle = [[((i + 1) % run) * count_y + j for i in range(run) for j in range(count_y)]]
    part = lax.all_to_all(sums.reshape(near, piece, width), ("zl", "gy"), 0, 0, axis_index_groups=middle)
    from_y = lax.ppermute(edge, "gy", forth)
    part = call(functools.partial(sum_parts, 1.0), jax.ShapeDtypeStruct((far, piece, width), BF), part)
    part = lax.all_to_all(part, "zh", 0, 0, axis_index_groups=[[(i + far // 2) % far for i in range(far)]])
    keep, send = call(add_edge, (rows_of(3, extent_y, dtype=F32), rows_of(3, extent_y)), inner, from_y)
    part, send = lax.optimization_barrier((part, send))
    from_x = lax.ppermute(send, gx_axes, up)
    part = call(functools.partial(sum_parts, scale), jax.ShapeDtypeStruct((near, piece, width), BF), part)
    part = lax.all_to_all(part, ("zl", "gy"), 0, 0, axis_index_groups=middle)
    whole, bias_grad = call(
        unpack_sums,
        (jax.ShapeDtypeStruct((TAPS * chans, width), F32), jax.ShapeDtypeStruct((1, chans), F32)),
        place,
        part,
        specs=[smem, vmem],
    )
    weight_grad = jnp.transpose(whole.reshape(TAPS, chans, width), (0, 2, 1))
    block = jax.ShapeDtypeStruct(features.shape, BF)
    output, input_grad = call(finish, (block, block), keep, from_x)
    return output, input_grad, weight_grad, bias_grad.reshape(chans)


def solution(mesh):
    split = Mesh(mesh.devices.reshape(8, 8, 2, 4), ("chan", "zh", "zl", "gy"))
    block = P("chan", ("zh", "zl"), "gy", None)
    return jax.shard_map(
        on_device,
        mesh=split,
        in_specs=(block, P(), P("chan"), block),
        out_specs=(block, block, P(None, None, "chan"), P("chan")),
        check_vma=False,
    )
```

```python
import functools

import jax
import jax.numpy as jnp
from jax import lax
from jax.experimental import pallas as pl
from jax.experimental.pallas import tpu as pltpu
from jax.sharding import Mesh, PartitionSpec as P

BF = jnp.bfloat16
F32 = jnp.float32
LANE = 128
TAPS = 27


def pack_block(features_hbm, cotangent_hbm, bias_hbm, out, x_send, y_send, features, cotangent, bias, arrived):
    copies = [
        pltpu.make_async_copy(source, target, arrived.at[n])
        for n, (source, target) in enumerate(
            ((features_hbm, features), (cotangent_hbm, cotangent), (bias_hbm, bias))
        )
    ]
    for copy in copies:
        copy.start()
    for copy in copies:
        copy.wait()
    cells = 2 * 8
    for x in range(2):
        rows = jnp.swapaxes(features[:, x].astype(F32), 0, 1).astype(BF)
        x_send[x * 8 : (x + 1) * 8] = rows
        for p in range(out.shape[0]):
            out[p, x * 8 : (x + 1) * 8] = rows
    x_send[cells:] = jnp.swapaxes(cotangent[:, 0].astype(F32), 0, 1).astype(BF)
    rows = jnp.swapaxes(cotangent[:, 1].astype(F32), 0, 1).astype(BF)
    y_send[...] = rows[0:1]
    chans = bias.shape[1]
    line = lax.broadcasted_iota(jnp.int32, (chans, chans), 0)
    lane = lax.broadcasted_iota(jnp.int32, (chans, chans), 1)
    column = jnp.sum(jnp.where(line == lane, jnp.broadcast_to(bias[...], (chans, chans)), 0.0), axis=1, keepdims=True)
    first = column.astype(BF).astype(F32)
    second = (column - first).astype(BF).astype(F32)
    third = column - first - second
    lane = lax.broadcasted_iota(jnp.int32, (chans, LANE), 1)
    parts = jnp.where(lane == 0, first, jnp.where(lane == 1, second, jnp.where(lane == 2, third, 0.0)))
    for p in range(out.shape[0]):
        out[p, cells] = parts.astype(BF)
        out[p, cells + 1 :] = rows[1:]


def pack_edge(own, from_x, out):
    out[0:2] = from_x[0:2]
    out[2:4] = from_x[8:10]
    out[4:5] = own[...]
    out[5:6] = from_x[16:17]


def pack_layer(from_x, from_y, out):
    for p in range(out.shape[0]):
        out[p, 0:8] = from_x[0:8]
        out[p, 8:15] = from_x[17:24]
        out[p, 15:21] = from_y[...]


def add_edge(inner, from_y, keep, send):
    for plane in range(6):
        grad_plane = plane < 4
        rows = 2 if grad_plane else 1
        start = 2 * plane if grad_plane else 8 + plane - 4
        values = inner[plane]
        added = from_y[start : start + rows].astype(F32)
        values = jnp.concatenate([values[0:rows] + added, values[rows:]], axis=0)
        if plane in (0, 1, 4):
            keep[min(plane, 2)] = values
        else:
            send[min(plane - 2, 2)] = values.astype(BF)


def finish(keep, from_x, output, input_grad):
    for x in range(2):
        input_grad[:, x] = jnp.swapaxes(keep[x] + from_x[x].astype(F32), 0, 1).astype(BF)
    output[:, 0] = jnp.swapaxes(from_x[2].astype(F32), 0, 1).astype(BF)
    output[:, 1] = jnp.swapaxes(keep[2], 0, 1).astype(BF)


def sum_parts(scale, parts, out):
    total = jnp.sum(parts[...].astype(F32), axis=0)
    if scale != 1.0:
        total = total * jnp.float32(scale)
    for p in range(out.shape[0]):
        out[p] = total.astype(BF)


def unpack_sums(place, parts, weight_out, bias_out):
    piece = parts.shape[1]
    rows, width = weight_out.shape
    chans = bias_out.shape[1]
    for n in range(parts.shape[0]):
        start = n * piece
        values = parts[n].astype(F32)
        if start + piece <= rows:
            weight_out[start : start + piece] = values
        elif start <= rows:
            if start < rows:
                weight_out[start:rows] = values[: rows - start]
            line = values[rows - start : rows - start + 1]
            bias_out[...] = pltpu.roll(line, lax.rem(width - place[0] * chans, width), 1)[:, :chans]


def conv_kernel(place, got, layer, beside, across, weight, own_weight, sums_ref, inner_ref, edge_ref, moved, grad, patch, spread, act):
    chan = place[0]
    peers, _, chans, _ = got.shape
    width = peers * chans
    own = pl.multiple_of(chan * chans, chans)

    def row(ref, index):
        return jnp.concatenate([ref[p, index] for p in range(peers)], axis=0)

    def feature(x, y):
        if y >= 8:
            return row(beside, 2 * x + y - 8) if x < 2 else row(layer, 15 + 2 * (x - 2) + y - 8)
        return row((got, got, layer, across)[x], 8 * (x % 2) * (x < 2) + y)

    def cotangent(x, y):
        if y == 7:
            return row(layer, 19 + x)
        return row(layer, 8 + y) if x else row(got, 17 + y)

    for x in range(4):
        for y in range(10):
            tile = feature(x, y)
            lanes = slice(y * LANE, (y + 1) * LANE)
            wide = tile.astype(F32)
            moved[x, 0:width, lanes] = pltpu.roll(wide, 1, 1).astype(BF)
            moved[x, width : 2 * width, lanes] = tile
            moved[x, 2 * width : 3 * width, lanes] = pltpu.roll(wide, LANE - 1, 1).astype(BF)

    bias = jnp.sum(row(got, 16).astype(F32), axis=1, keepdims=True)
    filters = jnp.concatenate([weight[t] for t in range(TAPS)], axis=1)
    half = 4
    for x in range(2):
        for part in range(8 // half):
            y0 = part * half
            span = half * LANE
            cells = jnp.concatenate(
                [moved[x + a, :, (b + y0) * LANE : (b + y0) * LANE + span] for a in range(3) for b in range(3)],
                axis=0,
            )
            pre = jnp.dot(filters, cells, preferred_element_type=F32) + bias
            sigma = jax.nn.sigmoid(pre)
            cot = jnp.concatenate([cotangent(x, y0 + y) for y in range(half)], axis=1).astype(F32)
            lanes = slice((x * 8 + y0) * LANE, (x * 8 + y0) * LANE + span)
            grad[:, lanes] = (cot * sigma * (1.0 + pre * (1.0 - sigma))).astype(BF)
            act[:, lanes] = (pre * sigma).astype(BF)
    for x in range(2):
        inner_ref[4 + x, 0] = jnp.zeros((chans, LANE), F32)
        for y in range(8):
            lanes = slice((x * 8 + y) * LANE, (x * 8 + y + 1) * LANE)
            tile = act[pl.ds(own, chans), lanes]
            if y == 7:
                edge_ref[8 + x] = tile
            else:
                inner_ref[4 + x, y + 1] = tile.astype(F32)

    for a in range(3):
        for b in range(3):
            for c in range(3):
                t = 9 * a + 3 * b + c
                for x in range(2):
                    patch[t * chans : (t + 1) * chans, x * 1024 : (x + 1) * 1024] = moved[
                        x + a, pl.ds(pl.multiple_of(c * width + own, chans), chans), b * LANE : (b + 8) * LANE
                    ]
    spare = patch.shape[0] - TAPS * chans
    index = lax.broadcasted_iota(jnp.int32, (spare, patch.shape[1]), 0)
    patch[TAPS * chans :, :] = jnp.where(index == 0, 1.0, 0.0).astype(BF)
    sums_ref[...] = lax.dot_general(
        patch[...], grad[...], (((1,), (1,)), ((), ())), preferred_element_type=F32
    ).astype(BF)

    spread[...] = jnp.zeros(spread.shape, F32)
    for x in range(2):
        terms = jnp.dot(own_weight[...], grad[:, x * 1024 : (x + 1) * 1024], preferred_element_type=F32)
        for a in range(3):
            for b in range(3):
                for c in range(3):
                    t = 9 * a + 3 * b + c
                    spread[c, x + a, :, b * LANE : (b + 8) * LANE] += terms[t * chans : (t + 1) * chans]
    for x in range(4):
        for y in range(10):
            lanes = slice(y * LANE, (y + 1) * LANE)
            tile = (
                pltpu.roll(spread[0, x, :, lanes], LANE - 1, 1)
                + spread[1, x, :, lanes]
                + pltpu.roll(spread[2, x, :, lanes], 1, 1)
            )
            if y >= 8:
                edge_ref[2 * x + y - 8] = tile.astype(BF)
            else:
                inner_ref[x, y] = tile


def on_device(features, weight, bias, cotangent):
    chans, extent_x, extent_y, depth = features.shape
    width = weight.shape[1]
    peers = width // chans
    chan = lax.axis_index("chan")
    count_x = lax.axis_size("zh") * lax.axis_size("zl")
    count_y = lax.axis_size("gy")
    gx_axes = ("zh", "zl")
    up = [(i, (i + 1) % count_x) for i in range(count_x)]
    down = [(i, (i - 1) % count_x) for i in range(count_x)]

    vmem = pl.BlockSpec(memory_space=pltpu.VMEM)
    smem = pl.BlockSpec(memory_space=pltpu.SMEM)

    def call(body, out_shape, *operands, specs=None):
        return pl.pallas_call(
            body,
            out_shape=out_shape,
            in_specs=specs or [vmem] * len(operands),
            out_specs=jax.tree.map(lambda _: vmem, out_shape),
            compiler_params=pltpu.CompilerParams(vmem_limit_bytes=16 * 1024 * 1024),
        )(*operands)

    def rows_of(*shape, dtype=BF):
        return jax.ShapeDtypeStruct((*shape, chans, depth), dtype)

    anywhere = pl.BlockSpec(memory_space=pl.ANY)
    parcel, x_send, y_send = pl.pallas_call(
        pack_block,
        out_shape=(rows_of(peers, 24), rows_of(24), rows_of(1)),
        in_specs=[anywhere] * 3,
        out_specs=(vmem,) * 3,
        scratch_shapes=[
            pltpu.VMEM(features.shape, BF),
            pltpu.VMEM(features.shape, BF),
            pltpu.VMEM((1, chans), F32),
            pltpu.SemaphoreType.DMA((3,)),
        ],
        compiler_params=pltpu.CompilerParams(vmem_limit_bytes=60 * 1024 * 1024),
    )(features, cotangent, bias.reshape(1, chans))
    got = lax.all_to_all(parcel, "chan", 0, 0)

    forth = [(i, (i + 1) % count_y) for i in range(count_y)]
    back = [(i, (i - 1) % count_y) for i in range(count_y)]
    from_x = lax.ppermute(x_send, gx_axes, down)
    from_y = lax.ppermute(call(pack_edge, rows_of(6), y_send, from_x), "gy", back)
    parcel = call(pack_layer, rows_of(peers, 21), from_x, from_y)
    parcel, got = lax.optimization_barrier((parcel, got))
    layer = lax.all_to_all(parcel, "chan", 0, 0)
    across = lax.ppermute(got[:, 8:16], gx_axes, down)
    beside = lax.ppermute(jnp.concatenate([got[:, 0:2], got[:, 8:10]], axis=1), "gy", back)
    own_weight = lax.dynamic_slice_in_dim(weight, chan * chans, chans, 2)
    own_weight = jnp.transpose(own_weight, (0, 2, 1)).reshape(TAPS * chans, width)

    cells = extent_x * extent_y * depth
    near = lax.axis_size("zl") * count_y
    piece = -(-(TAPS * chans + 1) // (near * 8)) * 8
    place = chan.astype(jnp.int32).reshape(1)
    sums, inner, edge = pl.pallas_call(
        conv_kernel,
        out_shape=(
            jax.ShapeDtypeStruct((near * piece, width), BF),
            rows_of(6, extent_y, dtype=F32),
            rows_of(10),
        ),
        in_specs=[smem] + [vmem] * 6,
        out_specs=(vmem, vmem, vmem),
        scratch_shapes=[
            pltpu.VMEM((4, 3 * width, 10 * LANE), BF),
            pltpu.VMEM((width, cells), BF),
            pltpu.VMEM((near * piece, cells), BF),
            pltpu.VMEM((3, 4, chans, 10 * LANE), F32),
            pltpu.VMEM((width, cells), BF),
        ],
        compiler_params=pltpu.CompilerParams(vmem_limit_bytes=40 * 1024 * 1024),
    )(place, got, layer, beside, across, weight, own_weight)

    scale = 1.0 / float(count_x * count_y * cells) ** 0.5
    far = lax.axis_size("zh")
    run = lax.axis_size("zl")
    middle = [[((i + 1) % run) * count_y + j for i in range(run) for j in range(count_y)]]
    part = lax.all_to_all(sums.reshape(near, piece, width), ("zl", "gy"), 0, 0, axis_index_groups=middle)
    from_y = lax.ppermute(edge, "gy", forth)
    part = call(functools.partial(sum_parts, 1.0), jax.ShapeDtypeStruct((far, piece, width), BF), part)
    part = lax.all_to_all(part, "zh", 0, 0, axis_index_groups=[[(i + far // 2) % far for i in range(far)]])
    keep, send = call(add_edge, (rows_of(3, extent_y, dtype=F32), rows_of(3, extent_y)), inner, from_y)
    part, send = lax.optimization_barrier((part, send))
    from_x = lax.ppermute(send, gx_axes, up)
    part = call(functools.partial(sum_parts, scale), jax.ShapeDtypeStruct((near, piece, width), BF), part)
    part = lax.all_to_all(part, ("zl", "gy"), 0, 0, axis_index_groups=middle)
    whole, bias_grad = call(
        unpack_sums,
        (jax.ShapeDtypeStruct((TAPS * chans, width), F32), jax.ShapeDtypeStruct((1, chans), F32)),
        place,
        part,
        specs=[smem, vmem],
    )
    whole, from_x = lax.optimization_barrier((whole, from_x))
    weight_grad = jnp.transpose(whole.reshape(TAPS, chans, width), (0, 2, 1))
    block = jax.ShapeDtypeStruct(features.shape, BF)
    output, input_grad = call(finish, (block, block), keep, from_x)
    return output, input_grad, weight_grad, bias_grad.reshape(chans)


def solution(mesh):
    split = Mesh(mesh.devices.reshape(8, 8, 2, 4), ("chan", "zh", "zl", "gy"))
    block = P("chan", ("zh", "zl"), "gy", None)
    return jax.shard_map(
        on_device,
        mesh=split,
        in_specs=(block, P(), P("chan"), block),
        out_specs=(block, block, P(None, None, "chan"), P("chan")),
        check_vma=False,
    )
```

```python
import functools

import jax
import jax.numpy as jnp
from jax import lax
from jax.experimental import pallas as pl
from jax.experimental.pallas import tpu as pltpu
from jax.sharding import Mesh, PartitionSpec as P

BF = jnp.bfloat16
F32 = jnp.float32
LANE = 128
TAPS = 27


def pack_block(features_hbm, cotangent_hbm, bias_hbm, out, x_send, y_send, features, cotangent, bias, arrived):
    copies = [
        pltpu.make_async_copy(source, target, arrived.at[n])
        for n, (source, target) in enumerate(
            ((features_hbm, features), (cotangent_hbm, cotangent), (bias_hbm, bias))
        )
    ]
    for copy in copies:
        copy.start()
    for copy in copies:
        copy.wait()
    cells = 2 * 8
    for x in range(2):
        rows = jnp.swapaxes(features[:, x].astype(F32), 0, 1).astype(BF)
        x_send[x * 8 : (x + 1) * 8] = rows
        for p in range(out.shape[0]):
            out[p, x * 8 : (x + 1) * 8] = rows
    x_send[cells:] = jnp.swapaxes(cotangent[:, 0].astype(F32), 0, 1).astype(BF)
    rows = jnp.swapaxes(cotangent[:, 1].astype(F32), 0, 1).astype(BF)
    y_send[...] = rows[0:1]
    chans = bias.shape[1]
    line = lax.broadcasted_iota(jnp.int32, (chans, chans), 0)
    lane = lax.broadcasted_iota(jnp.int32, (chans, chans), 1)
    column = jnp.sum(jnp.where(line == lane, jnp.broadcast_to(bias[...], (chans, chans)), 0.0), axis=1, keepdims=True)
    first = column.astype(BF).astype(F32)
    second = (column - first).astype(BF).astype(F32)
    third = column - first - second
    lane = lax.broadcasted_iota(jnp.int32, (chans, LANE), 1)
    parts = jnp.where(lane == 0, first, jnp.where(lane == 1, second, jnp.where(lane == 2, third, 0.0)))
    for p in range(out.shape[0]):
        out[p, cells] = parts.astype(BF)
        out[p, cells + 1 :] = rows[1:]


def pack_edge(own, from_x, out):
    out[0:2] = from_x[0:2]
    out[2:4] = from_x[8:10]
    out[4:5] = own[...]
    out[5:6] = from_x[16:17]


def pack_layer(from_x, from_y, out):
    for p in range(out.shape[0]):
        out[p, 0:6] = from_x[0:6]
        out[p, 6:13] = from_x[17:24]
        out[p, 13:19] = from_y[...]


def add_edge(inner, from_y, keep, send):
    for plane in range(6):
        grad_plane = plane < 4
        rows = 2 if grad_plane else 1
        start = 2 * plane if grad_plane else 8 + plane - 4
        values = inner[plane]
        added = from_y[start : start + rows].astype(F32)
        values = jnp.concatenate([values[0:rows] + added, values[rows:]], axis=0)
        if plane in (0, 1, 4):
            keep[min(plane, 2)] = values
        else:
            send[min(plane - 2, 2)] = values.astype(BF)


def finish(keep, from_x, output, input_grad):
    for x in range(2):
        input_grad[:, x] = jnp.swapaxes(keep[x] + from_x[x].astype(F32), 0, 1).astype(BF)
    output[:, 0] = jnp.swapaxes(from_x[2].astype(F32), 0, 1).astype(BF)
    output[:, 1] = jnp.swapaxes(keep[2], 0, 1).astype(BF)


def sum_parts(scale, parts, out):
    total = jnp.sum(parts[...].astype(F32), axis=0)
    if scale != 1.0:
        total = total * jnp.float32(scale)
    for p in range(out.shape[0]):
        out[p] = total.astype(BF)


def unpack_sums(place, parts, weight_out, bias_out):
    piece = parts.shape[1]
    rows, width = weight_out.shape
    chans = bias_out.shape[1]
    for n in range(parts.shape[0]):
        start = n * piece
        values = parts[n].astype(F32)
        if start + piece <= rows:
            weight_out[start : start + piece] = values
        elif start <= rows:
            if start < rows:
                weight_out[start:rows] = values[: rows - start]
            line = values[rows - start : rows - start + 1]
            bias_out[...] = pltpu.roll(line, lax.rem(width - place[0] * chans, width), 1)[:, :chans]


def conv_kernel(place, got, layer, beside, across, weight, own_weight, sums_ref, inner_ref, edge_ref, moved, grad, patch, spread, act):
    chan = place[0]
    peers, _, chans, _ = got.shape
    width = peers * chans
    own = pl.multiple_of(chan * chans, chans)

    def row(ref, index):
        return jnp.concatenate([ref[p, index] for p in range(peers)], axis=0)

    def feature(x, y):
        if y >= 8:
            return row(beside, 2 * x + y - 8) if x < 2 else row(layer, 13 + 2 * (x - 2) + y - 8)
        if x < 2:
            return row(got, x * 8 + y)
        return row(layer, y) if x == 2 and y < 6 else row(across, (x - 2) * 8 + y - 6)

    def cotangent(x, y):
        if y == 7:
            return row(layer, 17 + x)
        return row(layer, 6 + y) if x else row(got, 17 + y)

    for x in range(4):
        for y in range(10):
            tile = feature(x, y)
            lanes = slice(y * LANE, (y + 1) * LANE)
            wide = tile.astype(F32)
            moved[x, 0:width, lanes] = pltpu.roll(wide, 1, 1).astype(BF)
            moved[x, width : 2 * width, lanes] = tile
            moved[x, 2 * width : 3 * width, lanes] = pltpu.roll(wide, LANE - 1, 1).astype(BF)

    bias = jnp.sum(row(got, 16).astype(F32), axis=1, keepdims=True)
    filters = jnp.concatenate([weight[t] for t in range(TAPS)], axis=1)
    half = 4
    for x in range(2):
        for part in range(8 // half):
            y0 = part * half
            span = half * LANE
            cells = jnp.concatenate(
                [moved[x + a, :, (b + y0) * LANE : (b + y0) * LANE + span] for a in range(3) for b in range(3)],
                axis=0,
            )
            pre = jnp.dot(filters, cells, preferred_element_type=F32) + bias
            sigma = jax.nn.sigmoid(pre)
            cot = jnp.concatenate([cotangent(x, y0 + y) for y in range(half)], axis=1).astype(F32)
            lanes = slice((x * 8 + y0) * LANE, (x * 8 + y0) * LANE + span)
            grad[:, lanes] = (cot * sigma * (1.0 + pre * (1.0 - sigma))).astype(BF)
            act[:, lanes] = (pre * sigma).astype(BF)
    for x in range(2):
        inner_ref[4 + x, 0] = jnp.zeros((chans, LANE), F32)
        for y in range(8):
            lanes = slice((x * 8 + y) * LANE, (x * 8 + y + 1) * LANE)
            tile = act[pl.ds(own, chans), lanes]
            if y == 7:
                edge_ref[8 + x] = tile
            else:
                inner_ref[4 + x, y + 1] = tile.astype(F32)

    for a in range(3):
        for b in range(3):
            for c in range(3):
                t = 9 * a + 3 * b + c
                for x in range(2):
                    patch[t * chans : (t + 1) * chans, x * 1024 : (x + 1) * 1024] = moved[
                        x + a, pl.ds(pl.multiple_of(c * width + own, chans), chans), b * LANE : (b + 8) * LANE
                    ]
    spare = patch.shape[0] - TAPS * chans
    index = lax.broadcasted_iota(jnp.int32, (spare, patch.shape[1]), 0)
    patch[TAPS * chans :, :] = jnp.where(index == 0, 1.0, 0.0).astype(BF)
    sums_ref[...] = lax.dot_general(
        patch[...], grad[...], (((1,), (1,)), ((), ())), preferred_element_type=F32
    ).astype(BF)

    spread[...] = jnp.zeros(spread.shape, F32)
    for x in range(2):
        terms = jnp.dot(own_weight[...], grad[:, x * 1024 : (x + 1) * 1024], preferred_element_type=F32)
        for a in range(3):
            for b in range(3):
                for c in range(3):
                    t = 9 * a + 3 * b + c
                    spread[c, x + a, :, b * LANE : (b + 8) * LANE] += terms[t * chans : (t + 1) * chans]
    for x in range(4):
        for y in range(10):
            lanes = slice(y * LANE, (y + 1) * LANE)
            tile = (
                pltpu.roll(spread[0, x, :, lanes], LANE - 1, 1)
                + spread[1, x, :, lanes]
                + pltpu.roll(spread[2, x, :, lanes], 1, 1)
            )
            if y >= 8:
                edge_ref[2 * x + y - 8] = tile.astype(BF)
            else:
                inner_ref[x, y] = tile


def on_device(features, weight, bias, cotangent):
    chans, extent_x, extent_y, depth = features.shape
    width = weight.shape[1]
    peers = width // chans
    chan = lax.axis_index("chan")
    count_x = lax.axis_size("zh") * lax.axis_size("zl")
    count_y = lax.axis_size("gy")
    gx_axes = ("zh", "zl")
    up = [(i, (i + 1) % count_x) for i in range(count_x)]
    down = [(i, (i - 1) % count_x) for i in range(count_x)]

    vmem = pl.BlockSpec(memory_space=pltpu.VMEM)
    smem = pl.BlockSpec(memory_space=pltpu.SMEM)

    def call(body, out_shape, *operands, specs=None):
        return pl.pallas_call(
            body,
            out_shape=out_shape,
            in_specs=specs or [vmem] * len(operands),
            out_specs=jax.tree.map(lambda _: vmem, out_shape),
            compiler_params=pltpu.CompilerParams(vmem_limit_bytes=16 * 1024 * 1024),
        )(*operands)

    def rows_of(*shape, dtype=BF):
        return jax.ShapeDtypeStruct((*shape, chans, depth), dtype)

    anywhere = pl.BlockSpec(memory_space=pl.ANY)
    parcel, x_send, y_send = pl.pallas_call(
        pack_block,
        out_shape=(rows_of(peers, 24), rows_of(24), rows_of(1)),
        in_specs=[anywhere] * 3,
        out_specs=(vmem,) * 3,
        scratch_shapes=[
            pltpu.VMEM(features.shape, BF),
            pltpu.VMEM(features.shape, BF),
            pltpu.VMEM((1, chans), F32),
            pltpu.SemaphoreType.DMA((3,)),
        ],
        compiler_params=pltpu.CompilerParams(vmem_limit_bytes=60 * 1024 * 1024),
    )(features, cotangent, bias.reshape(1, chans))
    got = lax.all_to_all(parcel, "chan", 0, 0)

    forth = [(i, (i + 1) % count_y) for i in range(count_y)]
    back = [(i, (i - 1) % count_y) for i in range(count_y)]
    from_x = lax.ppermute(x_send, gx_axes, down)
    from_y = lax.ppermute(call(pack_edge, rows_of(6), y_send, from_x), "gy", back)
    parcel = call(pack_layer, rows_of(peers, 19), from_x, from_y)
    parcel, got = lax.optimization_barrier((parcel, got))
    layer = lax.all_to_all(parcel, "chan", 0, 0)
    across = lax.ppermute(got[:, 6:16], gx_axes, down)
    beside = lax.ppermute(jnp.concatenate([got[:, 0:2], got[:, 8:10]], axis=1), "gy", back)
    own_weight = lax.dynamic_slice_in_dim(weight, chan * chans, chans, 2)
    own_weight = jnp.transpose(own_weight, (0, 2, 1)).reshape(TAPS * chans, width)

    cells = extent_x * extent_y * depth
    near = lax.axis_size("zl") * count_y
    piece = -(-(TAPS * chans + 1) // (near * 8)) * 8
    place = chan.astype(jnp.int32).reshape(1)
    sums, inner, edge = pl.pallas_call(
        conv_kernel,
        out_shape=(
            jax.ShapeDtypeStruct((near * piece, width), BF),
            rows_of(6, extent_y, dtype=F32),
            rows_of(10),
        ),
        in_specs=[smem] + [vmem] * 6,
        out_specs=(vmem, vmem, vmem),
        scratch_shapes=[
            pltpu.VMEM((4, 3 * width, 10 * LANE), BF),
            pltpu.VMEM((width, cells), BF),
            pltpu.VMEM((near * piece, cells), BF),
            pltpu.VMEM((3, 4, chans, 10 * LANE), F32),
            pltpu.VMEM((width, cells), BF),
        ],
        compiler_params=pltpu.CompilerParams(vmem_limit_bytes=40 * 1024 * 1024),
    )(place, got, layer, beside, across, weight, own_weight)

    scale = 1.0 / float(count_x * count_y * cells) ** 0.5
    far = lax.axis_size("zh")
    run = lax.axis_size("zl")
    middle = [[((i + 1) % run) * count_y + j for i in range(run) for j in range(count_y)]]
    part = lax.all_to_all(sums.reshape(near, piece, width), ("zl", "gy"), 0, 0, axis_index_groups=middle)
    from_y = lax.ppermute(edge, "gy", forth)
    part = call(functools.partial(sum_parts, 1.0), jax.ShapeDtypeStruct((far, piece, width), BF), part)
    part = lax.all_to_all(part, "zh", 0, 0, axis_index_groups=[[(i + far // 2 + 1) % far for i in range(far)]])
    keep, send = call(add_edge, (rows_of(3, extent_y, dtype=F32), rows_of(3, extent_y)), inner, from_y)
    part, send = lax.optimization_barrier((part, send))
    from_x = lax.ppermute(send, gx_axes, up)
    part = call(functools.partial(sum_parts, scale), jax.ShapeDtypeStruct((near, piece, width), BF), part)
    part = lax.all_to_all(part, ("zl", "gy"), 0, 0, axis_index_groups=middle)
    whole, bias_grad = call(
        unpack_sums,
        (jax.ShapeDtypeStruct((TAPS * chans, width), F32), jax.ShapeDtypeStruct((1, chans), F32)),
        place,
        part,
        specs=[smem, vmem],
    )
    whole, from_x = lax.optimization_barrier((whole, from_x))
    weight_grad = jnp.transpose(whole.reshape(TAPS, chans, width), (0, 2, 1))
    block = jax.ShapeDtypeStruct(features.shape, BF)
    output, input_grad = call(finish, (block, block), keep, from_x)
    return output, input_grad, weight_grad, bias_grad.reshape(chans)


def solution(mesh):
    split = Mesh(mesh.devices.reshape(8, 8, 2, 4), ("chan", "zh", "zl", "gy"))
    block = P("chan", ("zh", "zl"), "gy", None)
    return jax.shard_map(
        on_device,
        mesh=split,
        in_specs=(block, P(), P("chan"), block),
        out_specs=(block, block, P(None, None, "chan"), P("chan")),
        check_vma=False,
    )
```

```python
import functools

import jax
import jax.numpy as jnp
from jax import lax
from jax.experimental import pallas as pl
from jax.experimental.pallas import tpu as pltpu
from jax.sharding import Mesh, PartitionSpec as P

BF = jnp.bfloat16
F32 = jnp.float32
LANE = 128
TAPS = 27


def pack_block(features_hbm, cotangent_hbm, bias_hbm, out, x_send, y_send, features, cotangent, bias, arrived):
    copies = [
        pltpu.make_async_copy(source, target, arrived.at[n])
        for n, (source, target) in enumerate(
            ((features_hbm, features), (cotangent_hbm, cotangent), (bias_hbm, bias))
        )
    ]
    for copy in copies:
        copy.start()
    for copy in copies:
        copy.wait()
    cells = 2 * 8
    for x in range(2):
        rows = jnp.swapaxes(features[:, x].astype(F32), 0, 1).astype(BF)
        if x == 0:
            x_send[0:6] = rows[0:6]
        else:
            x_send[6:8] = rows[0:2]
        for p in range(out.shape[0]):
            out[p, x * 8 : (x + 1) * 8] = rows
    x_send[8:16] = jnp.swapaxes(cotangent[:, 0].astype(F32), 0, 1).astype(BF)
    rows = jnp.swapaxes(cotangent[:, 1].astype(F32), 0, 1).astype(BF)
    y_send[...] = rows[0:1]
    chans = bias.shape[1]
    line = lax.broadcasted_iota(jnp.int32, (chans, chans), 0)
    lane = lax.broadcasted_iota(jnp.int32, (chans, chans), 1)
    column = jnp.sum(jnp.where(line == lane, jnp.broadcast_to(bias[...], (chans, chans)), 0.0), axis=1, keepdims=True)
    first = column.astype(BF).astype(F32)
    second = (column - first).astype(BF).astype(F32)
    third = column - first - second
    lane = lax.broadcasted_iota(jnp.int32, (chans, LANE), 1)
    parts = jnp.where(lane == 0, first, jnp.where(lane == 1, second, jnp.where(lane == 2, third, 0.0)))
    for p in range(out.shape[0]):
        out[p, cells] = parts.astype(BF)
        out[p, cells + 1 :] = rows[1:]


def pack_edge(own, from_x, out):
    out[0:2] = from_x[0:2]
    out[2:4] = from_x[6:8]
    out[4:5] = own[...]
    out[5:6] = from_x[8:9]


def pack_layer(from_x, from_y, out):
    for p in range(out.shape[0]):
        out[p, 0:6] = from_x[0:6]
        out[p, 6:13] = from_x[9:16]
        out[p, 13:19] = from_y[...]


def add_edge(inner, from_y, keep, send):
    for plane in range(6):
        grad_plane = plane < 4
        rows = 2 if grad_plane else 1
        start = 2 * plane if grad_plane else 8 + plane - 4
        values = inner[plane]
        added = from_y[start : start + rows].astype(F32)
        values = jnp.concatenate([values[0:rows] + added, values[rows:]], axis=0)
        if plane in (0, 1, 4):
            keep[min(plane, 2)] = values
        else:
            send[min(plane - 2, 2)] = values.astype(BF)


def finish(keep, from_x, output, input_grad):
    for x in range(2):
        input_grad[:, x] = jnp.swapaxes(keep[x] + from_x[x].astype(F32), 0, 1).astype(BF)
    output[:, 0] = jnp.swapaxes(from_x[2].astype(F32), 0, 1).astype(BF)
    output[:, 1] = jnp.swapaxes(keep[2], 0, 1).astype(BF)


def sum_parts(scale, parts, out):
    total = jnp.sum(parts[...].astype(F32), axis=0)
    if scale != 1.0:
        total = total * jnp.float32(scale)
    for p in range(out.shape[0]):
        out[p] = total.astype(BF)


def unpack_sums(place, parts, weight_out, bias_out):
    piece = parts.shape[1]
    rows, width = weight_out.shape
    chans = bias_out.shape[1]
    for n in range(parts.shape[0]):
        start = n * piece
        values = parts[n].astype(F32)
        if start + piece <= rows:
            weight_out[start : start + piece] = values
        elif start <= rows:
            if start < rows:
                weight_out[start:rows] = values[: rows - start]
            line = values[rows - start : rows - start + 1]
            bias_out[...] = pltpu.roll(line, lax.rem(width - place[0] * chans, width), 1)[:, :chans]


def conv_kernel(place, got, layer, beside, across, weight, own_weight, sums_ref, inner_ref, edge_ref, moved, grad, patch, spread, act):
    chan = place[0]
    peers, _, chans, _ = got.shape
    width = peers * chans
    own = pl.multiple_of(chan * chans, chans)

    def row(ref, index):
        return jnp.concatenate([ref[p, index] for p in range(peers)], axis=0)

    def feature(x, y):
        if y >= 8:
            return row(beside, 2 * x + y - 8) if x < 2 else row(layer, 13 + 2 * (x - 2) + y - 8)
        if x < 2:
            return row(got, x * 8 + y)
        return row(layer, y) if x == 2 and y < 6 else row(across, (x - 2) * 8 + y - 6)

    def cotangent(x, y):
        if y == 7:
            return row(layer, 17 + x)
        return row(layer, 6 + y) if x else row(got, 17 + y)

    for x in range(4):
        for y in range(10):
            tile = feature(x, y)
            lanes = slice(y * LANE, (y + 1) * LANE)
            wide = tile.astype(F32)
            moved[x, 0:width, lanes] = pltpu.roll(wide, 1, 1).astype(BF)
            moved[x, width : 2 * width, lanes] = tile
            moved[x, 2 * width : 3 * width, lanes] = pltpu.roll(wide, LANE - 1, 1).astype(BF)

    bias = jnp.sum(row(got, 16).astype(F32), axis=1, keepdims=True)
    filters = jnp.concatenate([weight[t] for t in range(TAPS)], axis=1)
    half = 4
    for x in range(2):
        for part in range(8 // half):
            y0 = part * half
            span = half * LANE
            cells = jnp.concatenate(
                [moved[x + a, :, (b + y0) * LANE : (b + y0) * LANE + span] for a in range(3) for b in range(3)],
                axis=0,
            )
            pre = jnp.dot(filters, cells, preferred_element_type=F32) + bias
            sigma = jax.nn.sigmoid(pre)
            cot = jnp.concatenate([cotangent(x, y0 + y) for y in range(half)], axis=1).astype(F32)
            lanes = slice((x * 8 + y0) * LANE, (x * 8 + y0) * LANE + span)
            grad[:, lanes] = (cot * sigma * (1.0 + pre * (1.0 - sigma))).astype(BF)
            act[:, lanes] = (pre * sigma).astype(BF)
    for x in range(2):
        inner_ref[4 + x, 0] = jnp.zeros((chans, LANE), F32)
        for y in range(8):
            lanes = slice((x * 8 + y) * LANE, (x * 8 + y + 1) * LANE)
            tile = act[pl.ds(own, chans), lanes]
            if y == 7:
                edge_ref[8 + x] = tile
            else:
                inner_ref[4 + x, y + 1] = tile.astype(F32)

    for a in range(3):
        for b in range(3):
            for c in range(3):
                t = 9 * a + 3 * b + c
                for x in range(2):
                    patch[t * chans : (t + 1) * chans, x * 1024 : (x + 1) * 1024] = moved[
                        x + a, pl.ds(pl.multiple_of(c * width + own, chans), chans), b * LANE : (b + 8) * LANE
                    ]
    spare = patch.shape[0] - TAPS * chans
    index = lax.broadcasted_iota(jnp.int32, (spare, patch.shape[1]), 0)
    patch[TAPS * chans :, :] = jnp.where(index == 0, 1.0, 0.0).astype(BF)
    sums_ref[...] = lax.dot_general(
        patch[...], grad[...], (((1,), (1,)), ((), ())), preferred_element_type=F32
    ).astype(BF)

    spread[...] = jnp.zeros(spread.shape, F32)
    for x in range(2):
        terms = jnp.dot(own_weight[...], grad[:, x * 1024 : (x + 1) * 1024], preferred_element_type=F32)
        for a in range(3):
            for b in range(3):
                for c in range(3):
                    t = 9 * a + 3 * b + c
                    spread[c, x + a, :, b * LANE : (b + 8) * LANE] += terms[t * chans : (t + 1) * chans]
    for x in range(4):
        for y in range(10):
            lanes = slice(y * LANE, (y + 1) * LANE)
            tile = (
                pltpu.roll(spread[0, x, :, lanes], LANE - 1, 1)
                + spread[1, x, :, lanes]
                + pltpu.roll(spread[2, x, :, lanes], 1, 1)
            )
            if y >= 8:
                edge_ref[2 * x + y - 8] = tile.astype(BF)
            else:
                inner_ref[x, y] = tile


def on_device(features, weight, bias, cotangent):
    chans, extent_x, extent_y, depth = features.shape
    width = weight.shape[1]
    peers = width // chans
    chan = lax.axis_index("chan")
    count_x = lax.axis_size("zh") * lax.axis_size("zl")
    count_y = lax.axis_size("gy")
    gx_axes = ("zh", "zl")
    up = [(i, (i + 1) % count_x) for i in range(count_x)]
    down = [(i, (i - 1) % count_x) for i in range(count_x)]

    vmem = pl.BlockSpec(memory_space=pltpu.VMEM)
    smem = pl.BlockSpec(memory_space=pltpu.SMEM)

    def call(body, out_shape, *operands, specs=None):
        return pl.pallas_call(
            body,
            out_shape=out_shape,
            in_specs=specs or [vmem] * len(operands),
            out_specs=jax.tree.map(lambda _: vmem, out_shape),
            compiler_params=pltpu.CompilerParams(vmem_limit_bytes=16 * 1024 * 1024),
        )(*operands)

    def rows_of(*shape, dtype=BF):
        return jax.ShapeDtypeStruct((*shape, chans, depth), dtype)

    anywhere = pl.BlockSpec(memory_space=pl.ANY)
    parcel, x_send, y_send = pl.pallas_call(
        pack_block,
        out_shape=(rows_of(peers, 24), rows_of(16), rows_of(1)),
        in_specs=[anywhere] * 3,
        out_specs=(vmem,) * 3,
        scratch_shapes=[
            pltpu.VMEM(features.shape, BF),
            pltpu.VMEM(features.shape, BF),
            pltpu.VMEM((1, chans), F32),
            pltpu.SemaphoreType.DMA((3,)),
        ],
        compiler_params=pltpu.CompilerParams(vmem_limit_bytes=60 * 1024 * 1024),
    )(features, cotangent, bias.reshape(1, chans))
    got = lax.all_to_all(parcel, "chan", 0, 0)

    forth = [(i, (i + 1) % count_y) for i in range(count_y)]
    back = [(i, (i - 1) % count_y) for i in range(count_y)]
    from_x = lax.ppermute(x_send, gx_axes, down)
    from_y = lax.ppermute(call(pack_edge, rows_of(6), y_send, from_x), "gy", back)
    parcel = call(pack_layer, rows_of(peers, 19), from_x, from_y)
    parcel, got = lax.optimization_barrier((parcel, got))
    layer = lax.all_to_all(parcel, "chan", 0, 0)
    across = lax.ppermute(got[:, 6:16], gx_axes, down)
    beside = lax.ppermute(jnp.concatenate([got[:, 0:2], got[:, 8:10]], axis=1), "gy", back)
    own_weight = lax.dynamic_slice_in_dim(weight, chan * chans, chans, 2)
    own_weight = jnp.transpose(own_weight, (0, 2, 1)).reshape(TAPS * chans, width)

    cells = extent_x * extent_y * depth
    near = lax.axis_size("zl") * count_y
    piece = -(-(TAPS * chans + 1) // (near * 8)) * 8
    place = chan.astype(jnp.int32).reshape(1)
    sums, inner, edge = pl.pallas_call(
        conv_kernel,
        out_shape=(
            jax.ShapeDtypeStruct((near * piece, width), BF),
            rows_of(6, extent_y, dtype=F32),
            rows_of(10),
        ),
        in_specs=[smem] + [vmem] * 6,
        out_specs=(vmem, vmem, vmem),
        scratch_shapes=[
            pltpu.VMEM((4, 3 * width, 10 * LANE), BF),
            pltpu.VMEM((width, cells), BF),
            pltpu.VMEM((near * piece, cells), BF),
            pltpu.VMEM((3, 4, chans, 10 * LANE), F32),
            pltpu.VMEM((width, cells), BF),
        ],
        compiler_params=pltpu.CompilerParams(vmem_limit_bytes=40 * 1024 * 1024),
    )(place, got, layer, beside, across, weight, own_weight)

    scale = 1.0 / float(count_x * count_y * cells) ** 0.5
    far = lax.axis_size("zh")
    run = lax.axis_size("zl")
    middle = [[((i + 1) % run) * count_y + j for i in range(run) for j in range(count_y)]]
    part = lax.all_to_all(sums.reshape(near, piece, width), ("zl", "gy"), 0, 0, axis_index_groups=middle)
    from_y = lax.ppermute(edge, "gy", forth)
    part = call(functools.partial(sum_parts, 1.0), jax.ShapeDtypeStruct((far, piece, width), BF), part)
    part = lax.all_to_all(part, "zh", 0, 0, axis_index_groups=[[(i + far // 2 + 1) % far for i in range(far)]])
    keep, send = call(add_edge, (rows_of(3, extent_y, dtype=F32), rows_of(3, extent_y)), inner, from_y)
    part, send = lax.optimization_barrier((part, send))
    from_x = lax.ppermute(send, gx_axes, up)
    part = call(functools.partial(sum_parts, scale), jax.ShapeDtypeStruct((near, piece, width), BF), part)
    part = lax.all_to_all(part, ("zl", "gy"), 0, 0, axis_index_groups=middle)
    whole, bias_grad = call(
        unpack_sums,
        (jax.ShapeDtypeStruct((TAPS * chans, width), F32), jax.ShapeDtypeStruct((1, chans), F32)),
        place,
        part,
        specs=[smem, vmem],
    )
    whole, from_x = lax.optimization_barrier((whole, from_x))
    weight_grad = jnp.transpose(whole.reshape(TAPS, chans, width), (0, 2, 1))
    block = jax.ShapeDtypeStruct(features.shape, BF)
    output, input_grad = call(finish, (block, block), keep, from_x)
    return output, input_grad, weight_grad, bias_grad.reshape(chans)


def solution(mesh):
    split = Mesh(mesh.devices.reshape(8, 8, 2, 4), ("chan", "zh", "zl", "gy"))
    block = P("chan", ("zh", "zl"), "gy", None)
    return jax.shard_map(
        on_device,
        mesh=split,
        in_specs=(block, P(), P("chan"), block),
        out_specs=(block, block, P(None, None, "chan"), P("chan")),
        check_vma=False,
    )
```

```python
import functools

import jax
import jax.numpy as jnp
from jax import lax
from jax.experimental import pallas as pl
from jax.experimental.pallas import tpu as pltpu
from jax.sharding import Mesh, PartitionSpec as P

BF = jnp.bfloat16
F32 = jnp.float32
LANE = 128
TAPS = 27


def pack_block(features_hbm, cotangent_hbm, bias_hbm, out, x_send, y_send, features, cotangent, bias, arrived):
    copies = [
        pltpu.make_async_copy(source, target, arrived.at[n])
        for n, (source, target) in enumerate(
            ((features_hbm, features), (cotangent_hbm, cotangent), (bias_hbm, bias))
        )
    ]
    for copy in copies:
        copy.start()
    for copy in copies:
        copy.wait()
    cells = 2 * 8
    for x in range(2):
        rows = jnp.swapaxes(features[:, x].astype(F32), 0, 1).astype(BF)
        if x == 0:
            x_send[0:7] = rows[0:7]
        else:
            x_send[7:9] = rows[0:2]
        for p in range(out.shape[0]):
            out[p, x * 8 : (x + 1) * 8] = rows
    x_send[9:17] = jnp.swapaxes(cotangent[:, 0].astype(F32), 0, 1).astype(BF)
    rows = jnp.swapaxes(cotangent[:, 1].astype(F32), 0, 1).astype(BF)
    y_send[...] = rows[0:1]
    chans = bias.shape[1]
    line = lax.broadcasted_iota(jnp.int32, (chans, chans), 0)
    lane = lax.broadcasted_iota(jnp.int32, (chans, chans), 1)
    column = jnp.sum(jnp.where(line == lane, jnp.broadcast_to(bias[...], (chans, chans)), 0.0), axis=1, keepdims=True)
    first = column.astype(BF).astype(F32)
    second = (column - first).astype(BF).astype(F32)
    third = column - first - second
    lane = lax.broadcasted_iota(jnp.int32, (chans, LANE), 1)
    parts = jnp.where(lane == 0, first, jnp.where(lane == 1, second, jnp.where(lane == 2, third, 0.0)))
    for p in range(out.shape[0]):
        out[p, cells] = parts.astype(BF)
        out[p, cells + 1 :] = rows[1:]


def pack_edge(own, from_x, out):
    out[0:2] = from_x[0:2]
    out[2:4] = from_x[7:9]
    out[4:5] = own[...]
    out[5:6] = from_x[9:10]


def pack_layer(from_x, from_y, out):
    for p in range(out.shape[0]):
        out[p, 0:7] = from_x[0:7]
        out[p, 7:14] = from_x[10:17]
        out[p, 14:20] = from_y[...]


def add_edge(inner, from_y, keep, send):
    for plane in range(6):
        grad_plane = plane < 4
        rows = 2 if grad_plane else 1
        start = 2 * plane if grad_plane else 8 + plane - 4
        values = inner[plane]
        added = from_y[start : start + rows].astype(F32)
        values = jnp.concatenate([values[0:rows] + added, values[rows:]], axis=0)
        if plane in (0, 1, 4):
            keep[min(plane, 2)] = values
        else:
            send[min(plane - 2, 2)] = values.astype(BF)


def finish(keep, from_x, output, input_grad):
    for x in range(2):
        input_grad[:, x] = jnp.swapaxes(keep[x] + from_x[x].astype(F32), 0, 1).astype(BF)
    output[:, 0] = jnp.swapaxes(from_x[2].astype(F32), 0, 1).astype(BF)
    output[:, 1] = jnp.swapaxes(keep[2], 0, 1).astype(BF)


def sum_parts(scale, parts, out):
    total = jnp.sum(parts[...].astype(F32), axis=0)
    if scale != 1.0:
        total = total * jnp.float32(scale)
    for p in range(out.shape[0]):
        out[p] = total.astype(BF)


def unpack_sums(place, parts, weight_out, bias_out):
    piece = parts.shape[1]
    rows, width = weight_out.shape
    chans = bias_out.shape[1]
    for n in range(parts.shape[0]):
        start = n * piece
        values = parts[n].astype(F32)
        if start + piece <= rows:
            weight_out[start : start + piece] = values
        elif start <= rows:
            if start < rows:
                weight_out[start:rows] = values[: rows - start]
            line = values[rows - start : rows - start + 1]
            bias_out[...] = pltpu.roll(line, lax.rem(width - place[0] * chans, width), 1)[:, :chans]


def conv_kernel(place, got, layer, beside, across, weight, own_weight, sums_ref, inner_ref, edge_ref, moved, grad, patch, spread, act):
    chan = place[0]
    peers, _, chans, _ = got.shape
    width = peers * chans
    own = pl.multiple_of(chan * chans, chans)

    def row(ref, index):
        return jnp.concatenate([ref[p, index] for p in range(peers)], axis=0)

    def feature(x, y):
        if y >= 8:
            return row(beside, 2 * x + y - 8) if x < 2 else row(layer, 14 + 2 * (x - 2) + y - 8)
        if x < 2:
            return row(got, x * 8 + y)
        return row(layer, y) if x == 2 and y < 7 else row(across, (x - 2) * 8 + y - 7)

    def cotangent(x, y):
        if y == 7:
            return row(layer, 18 + x)
        return row(layer, 7 + y) if x else row(got, 17 + y)

    for x in range(4):
        for y in range(10):
            tile = feature(x, y)
            lanes = slice(y * LANE, (y + 1) * LANE)
            wide = tile.astype(F32)
            moved[x, 0:width, lanes] = pltpu.roll(wide, 1, 1).astype(BF)
            moved[x, width : 2 * width, lanes] = tile
            moved[x, 2 * width : 3 * width, lanes] = pltpu.roll(wide, LANE - 1, 1).astype(BF)

    bias = jnp.sum(row(got, 16).astype(F32), axis=1, keepdims=True)
    filters = jnp.concatenate([weight[t] for t in range(TAPS)], axis=1)
    half = 4
    for x in range(2):
        for part in range(8 // half):
            y0 = part * half
            span = half * LANE
            cells = jnp.concatenate(
                [moved[x + a, :, (b + y0) * LANE : (b + y0) * LANE + span] for a in range(3) for b in range(3)],
                axis=0,
            )
            pre = jnp.dot(filters, cells, preferred_element_type=F32) + bias
            sigma = jax.nn.sigmoid(pre)
            cot = jnp.concatenate([cotangent(x, y0 + y) for y in range(half)], axis=1).astype(F32)
            lanes = slice((x * 8 + y0) * LANE, (x * 8 + y0) * LANE + span)
            grad[:, lanes] = (cot * sigma * (1.0 + pre * (1.0 - sigma))).astype(BF)
            act[:, lanes] = (pre * sigma).astype(BF)
    for x in range(2):
        inner_ref[4 + x, 0] = jnp.zeros((chans, LANE), F32)
        for y in range(8):
            lanes = slice((x * 8 + y) * LANE, (x * 8 + y + 1) * LANE)
            tile = act[pl.ds(own, chans), lanes]
            if y == 7:
                edge_ref[8 + x] = tile
            else:
                inner_ref[4 + x, y + 1] = tile.astype(F32)

    for a in range(3):
        for b in range(3):
            for c in range(3):
                t = 9 * a + 3 * b + c
                for x in range(2):
                    patch[t * chans : (t + 1) * chans, x * 1024 : (x + 1) * 1024] = moved[
                        x + a, pl.ds(pl.multiple_of(c * width + own, chans), chans), b * LANE : (b + 8) * LANE
                    ]
    spare = patch.shape[0] - TAPS * chans
    index = lax.broadcasted_iota(jnp.int32, (spare, patch.shape[1]), 0)
    patch[TAPS * chans :, :] = jnp.where(index == 0, 1.0, 0.0).astype(BF)
    sums_ref[...] = lax.dot_general(
        patch[...], grad[...], (((1,), (1,)), ((), ())), preferred_element_type=F32
    ).astype(BF)

    spread[...] = jnp.zeros(spread.shape, F32)
    for x in range(2):
        terms = jnp.dot(own_weight[...], grad[:, x * 1024 : (x + 1) * 1024], preferred_element_type=F32)
        for a in range(3):
            for b in range(3):
                for c in range(3):
                    t = 9 * a + 3 * b + c
                    spread[c, x + a, :, b * LANE : (b + 8) * LANE] += terms[t * chans : (t + 1) * chans]
    for x in range(4):
        for y in range(10):
            lanes = slice(y * LANE, (y + 1) * LANE)
            tile = (
                pltpu.roll(spread[0, x, :, lanes], LANE - 1, 1)
                + spread[1, x, :, lanes]
                + pltpu.roll(spread[2, x, :, lanes], 1, 1)
            )
            if y >= 8:
                edge_ref[2 * x + y - 8] = tile.astype(BF)
            else:
                inner_ref[x, y] = tile


def on_device(features, weight, bias, cotangent):
    chans, extent_x, extent_y, depth = features.shape
    width = weight.shape[1]
    peers = width // chans
    chan = lax.axis_index("chan")
    count_x = lax.axis_size("zh") * lax.axis_size("zl")
    count_y = lax.axis_size("gy")
    gx_axes = ("zh", "zl")
    up = [(i, (i + 1) % count_x) for i in range(count_x)]
    down = [(i, (i - 1) % count_x) for i in range(count_x)]

    vmem = pl.BlockSpec(memory_space=pltpu.VMEM)
    smem = pl.BlockSpec(memory_space=pltpu.SMEM)

    def call(body, out_shape, *operands, specs=None):
        return pl.pallas_call(
            body,
            out_shape=out_shape,
            in_specs=specs or [vmem] * len(operands),
            out_specs=jax.tree.map(lambda _: vmem, out_shape),
            compiler_params=pltpu.CompilerParams(vmem_limit_bytes=16 * 1024 * 1024),
        )(*operands)

    def rows_of(*shape, dtype=BF):
        return jax.ShapeDtypeStruct((*shape, chans, depth), dtype)

    anywhere = pl.BlockSpec(memory_space=pl.ANY)
    parcel, x_send, y_send = pl.pallas_call(
        pack_block,
        out_shape=(rows_of(peers, 24), rows_of(17), rows_of(1)),
        in_specs=[anywhere] * 3,
        out_specs=(vmem,) * 3,
        scratch_shapes=[
            pltpu.VMEM(features.shape, BF),
            pltpu.VMEM(features.shape, BF),
            pltpu.VMEM((1, chans), F32),
            pltpu.SemaphoreType.DMA((3,)),
        ],
        compiler_params=pltpu.CompilerParams(vmem_limit_bytes=60 * 1024 * 1024),
    )(features, cotangent, bias.reshape(1, chans))
    got = lax.all_to_all(parcel, "chan", 0, 0)

    forth = [(i, (i + 1) % count_y) for i in range(count_y)]
    back = [(i, (i - 1) % count_y) for i in range(count_y)]
    from_x = lax.ppermute(x_send, gx_axes, down)
    from_y = lax.ppermute(call(pack_edge, rows_of(6), y_send, from_x), "gy", back)
    parcel = call(pack_layer, rows_of(peers, 20), from_x, from_y)
    parcel, got = lax.optimization_barrier((parcel, got))
    layer = lax.all_to_all(parcel, "chan", 0, 0)
    across = lax.ppermute(got[:, 7:16], gx_axes, down)
    beside = lax.ppermute(jnp.concatenate([got[:, 0:2], got[:, 8:10]], axis=1), "gy", back)
    own_weight = lax.dynamic_slice_in_dim(weight, chan * chans, chans, 2)
    own_weight = jnp.transpose(own_weight, (0, 2, 1)).reshape(TAPS * chans, width)

    cells = extent_x * extent_y * depth
    near = lax.axis_size("zl") * count_y
    piece = -(-(TAPS * chans + 1) // (near * 8)) * 8
    place = chan.astype(jnp.int32).reshape(1)
    sums, inner, edge = pl.pallas_call(
        conv_kernel,
        out_shape=(
            jax.ShapeDtypeStruct((near * piece, width), BF),
            rows_of(6, extent_y, dtype=F32),
            rows_of(10),
        ),
        in_specs=[smem] + [vmem] * 6,
        out_specs=(vmem, vmem, vmem),
        scratch_shapes=[
            pltpu.VMEM((4, 3 * width, 10 * LANE), BF),
            pltpu.VMEM((width, cells), BF),
            pltpu.VMEM((near * piece, cells), BF),
            pltpu.VMEM((3, 4, chans, 10 * LANE), F32),
            pltpu.VMEM((width, cells), BF),
        ],
        compiler_params=pltpu.CompilerParams(vmem_limit_bytes=40 * 1024 * 1024),
    )(place, got, layer, beside, across, weight, own_weight)

    scale = 1.0 / float(count_x * count_y * cells) ** 0.5
    far = lax.axis_size("zh")
    run = lax.axis_size("zl")
    middle = [[((i + 1) % run) * count_y + j for i in range(run) for j in range(count_y)]]
    part = lax.all_to_all(sums.reshape(near, piece, width), ("zl", "gy"), 0, 0, axis_index_groups=middle)
    from_y = lax.ppermute(edge, "gy", forth)
    part = call(functools.partial(sum_parts, 1.0), jax.ShapeDtypeStruct((far, piece, width), BF), part)
    part = lax.all_to_all(part, "zh", 0, 0, axis_index_groups=[[(i + far // 2 + 1) % far for i in range(far)]])
    keep, send = call(add_edge, (rows_of(3, extent_y, dtype=F32), rows_of(3, extent_y)), inner, from_y)
    part, send = lax.optimization_barrier((part, send))
    from_x = lax.ppermute(send, gx_axes, up)
    part = call(functools.partial(sum_parts, scale), jax.ShapeDtypeStruct((near, piece, width), BF), part)
    part = lax.all_to_all(part, ("zl", "gy"), 0, 0, axis_index_groups=middle)
    whole, bias_grad = call(
        unpack_sums,
        (jax.ShapeDtypeStruct((TAPS * chans, width), F32), jax.ShapeDtypeStruct((1, chans), F32)),
        place,
        part,
        specs=[smem, vmem],
    )
    whole, from_x = lax.optimization_barrier((whole, from_x))
    weight_grad = jnp.transpose(whole.reshape(TAPS, chans, width), (0, 2, 1))
    block = jax.ShapeDtypeStruct(features.shape, BF)
    output, input_grad = call(finish, (block, block), keep, from_x)
    return output, input_grad, weight_grad, bias_grad.reshape(chans)


def solution(mesh):
    split = Mesh(mesh.devices.reshape(8, 8, 2, 4), ("chan", "zh", "zl", "gy"))
    block = P("chan", ("zh", "zl"), "gy", None)
    return jax.shard_map(
        on_device,
        mesh=split,
        in_specs=(block, P(), P("chan"), block),
        out_specs=(block, block, P(None, None, "chan"), P("chan")),
        check_vma=False,
    )
```
